256 devices in a mesh: frames: 32 (over z_hi, y, core), heads: 8 (over z_lo, x).
Axes of the slice: x: 4, y: 4, z: 8 (z_hi: 4, z_lo: 2; z = z_hi * 2 + z_lo), core: 2. Of those that a mesh axis runs over, the one named last changes fastest.
Arguments:
- span_qkv: bfloat16 [3, 2304, 5120], P(None, ('frames', 'heads')), may hold values from -64 to 64
- history_kv: bfloat16 [2, 6144, 5120], P(None, 'frames', 'heads'), may hold values from -4 to 4
Outputs:
- attended: bfloat16 [2304, 5120], P(('frames', 'heads'))
The draws below stay inside these ranges and needn't reach their ends.
All inputs are finite; a program needn't handle non-finite values.
Results may differ from the reference program's by a relative error of at most 0.017.
Values may be sent and summed in bfloat16 or wider, within the bound.
No kernel may reach another device: no remote copies, remote signals or barrier semaphores. Data moves between devices by JAX's collectives and lax.ppermute only.
A program may use at most 128 MiB of HBM per device.

```python
import math
import jax
import jax.numpy as jnp
from jax import lax

HEADS = 40
HEAD_DIM = 128
D = 5120
SPAN_FRAMES = 3
TOKENS = 2304
HIST = 6144


def draw_span_qkv(key, part):
    key = jax.random.fold_in(key, 11)
    first_key = jax.random.fold_in(key, 0)
    shape = (3, TOKENS, HEADS * HEAD_DIM)
    base = jnp.clip(jax.random.normal(first_key, shape, jnp.float32), -4.0, 4.0)
    queries = 2.5 * base[0]
    keys = base[1]
    values = base[2]
    return jnp.stack([queries, keys, values], 0).astype(jnp.bfloat16)


def block_levels(own_key, shape, cuts, low, high):
    loudness = 1.0
    for dim, parts in cuts:
        heights = jax.random.uniform(jax.random.fold_in(jax.random.fold_in(own_key, 6), dim), (parts,), jnp.float32, low / len(cuts), high / len(cuts))
        loudness = loudness * jnp.repeat(jnp.exp(heights), shape[dim] // parts).reshape((-1,) + (1,) * (len(shape) - 1 - dim))
    return loudness


def bell_draw(stream_key, extent, width, most, cuts=(), kind=jnp.bfloat16):
    array = width * jax.random.normal(stream_key, extent, jnp.float32)
    if cuts:
        array = array * block_levels(stream_key, extent, cuts, -0.22, 0.18)
    return jnp.clip(array, -most, most).astype(kind)


def setup_inputs(seed: int = 0) -> dict:
    key_of = jax.random.split(jax.random.key(seed), 3)
    span_qkv = draw_span_qkv(jax.random.fold_in(key_of[2], 71), 0)
    history_kv = bell_draw(key_of[1], (2, HIST, D), 1.0, 4.0, ((1, 32), (2, 8)))
    return {"span_qkv": span_qkv, "history_kv": history_kv}


def reference(span_qkv, history_kv):
    frame_len = TOKENS // SPAN_FRAMES
    scale = 1.0 / math.sqrt(HEAD_DIM)
    block = math.gcd(TOKENS, 512)
    key_frame = jnp.concatenate([jnp.full((HIST,), -1, jnp.int32), jnp.arange(TOKENS, dtype=jnp.int32) // frame_len])

    def one_head(head):
        start = (head * HEAD_DIM).astype(jnp.int32)
        keys = jnp.concatenate([lax.dynamic_slice_in_dim(history_kv[0], start, HEAD_DIM, 1), lax.dynamic_slice_in_dim(span_qkv[1], start, HEAD_DIM, 1)], 0)
        values = jnp.concatenate([lax.dynamic_slice_in_dim(history_kv[1], start, HEAD_DIM, 1), lax.dynamic_slice_in_dim(span_qkv[2], start, HEAD_DIM, 1)], 0)
        queries = lax.dynamic_slice_in_dim(span_qkv[0], start, HEAD_DIM, 1)

        def one_block(index):
            first = (index * block).astype(jnp.int32)
            query_block = lax.dynamic_slice_in_dim(queries, first, block, 0)
            query_frame = (first + jnp.arange(block, dtype=jnp.int32)) // frame_len
            score = jnp.dot(query_block, keys.T, preferred_element_type=jnp.float32) * scale
            score = jnp.where(query_frame[:, None] >= key_frame[None, :], score, -1e+30)
            largest = lax.optimization_barrier(jnp.max(score, axis=1, keepdims=True))
            weight = jnp.exp(score - largest)
            total = lax.optimization_barrier(jnp.sum(weight, axis=1, keepdims=True))
            summed = jnp.dot(weight.astype(jnp.bfloat16), values, preferred_element_type=jnp.float32)
            return (summed / total).astype(jnp.bfloat16)
        result = lax.map(one_block, jnp.arange(TOKENS // block, dtype=jnp.int32))
        return result.reshape(TOKENS, HEAD_DIM)
    every = lax.map(one_head, jnp.arange(HEADS, dtype=jnp.int32))
    return jnp.transpose(every, (1, 0, 2)).reshape(TOKENS, HEADS * HEAD_DIM)
```

```python
import math

import jax
import jax.numpy as jnp
from jax import lax
from jax.experimental import pallas as pl
from jax.experimental.pallas import tpu as pltpu
from jax.sharding import Mesh, PartitionSpec as P

HEADS = 40
HEAD_DIM = 128
TOKENS = 2304
HIST = 6144
FRAME_LEN = 768

FRAMES = ("zh", "y", "c")
GROUPS = ("zl", "x")
NZ, NY, NC, NG = 4, 4, 2, 8
HERE = HEADS // NG
WIDE = HERE * HEAD_DIM
HOME = TOKENS // (NZ * NY * NC * NG)
OWN = HOME * NG
PAD = 80
HKEYS = HIST // (NZ * NY * NC)
CHUNK = 48
ROWS = HERE * HOME
SENT = 32
SCALE = math.log2(math.e) / math.sqrt(HEAD_DIM)
F32, BF16 = jnp.float32, jnp.bfloat16
VMEM_LIMIT = 48 * 2**20


def params():
    return pltpu.CompilerParams(vmem_limit_bytes=VMEM_LIMIT)


def in_vmem(count):
    return [pl.BlockSpec(memory_space=pltpu.VMEM)] * count


def pack_kernel(x_ref, o_ref, scratch):
    scratch[...] = jnp.zeros_like(scratch)
    for g in range(NG):
        for i in range(3):
            piece = x_ref[i, :, g * WIDE : (g + 1) * WIDE]
            scratch[g, i * HOME : (i + 1) * HOME, :] = piece.astype(F32)
        o_ref[g] = scratch[g].astype(BF16)


def pack(x):
    return pl.pallas_call(
        pack_kernel,
        out_shape=jax.ShapeDtypeStruct((NG, SENT, WIDE), BF16),
        in_specs=in_vmem(1),
        out_specs=pl.BlockSpec(memory_space=pltpu.VMEM),
        scratch_shapes=[pltpu.VMEM((NG, SENT, WIDE), F32)],
        compiler_params=params(),
    )(x)


def unpack_kernel(x_ref, q_ref, kv_ref, scratch):
    scratch[...] = jnp.zeros_like(scratch)
    for g in range(NG):
        piece = x_ref[g].astype(F32)
        for i in range(3):
            scratch[i, g * HOME : (g + 1) * HOME, :] = piece[i * HOME : (i + 1) * HOME]
    q_ref[...] = scratch[0].astype(BF16)
    kv_ref[0] = scratch[1].astype(BF16)
    kv_ref[1] = scratch[2].astype(BF16)


def unpack(x):
    return pl.pallas_call(
        unpack_kernel,
        out_shape=(
            jax.ShapeDtypeStruct((PAD, WIDE), BF16),
            jax.ShapeDtypeStruct((2, PAD, WIDE), BF16),
        ),
        in_specs=in_vmem(1),
        out_specs=tuple(in_vmem(2)),
        scratch_shapes=[pltpu.VMEM((3, PAD, WIDE), F32)],
        compiler_params=params(),
    )(x)


QROWS = NZ * PAD
NHIST = NY * NC * HKEYS
NSPAN = NY * NC * PAD


def attend_kernel(place, *refs):
    qs = refs[:NZ]
    hist = refs[NZ : NZ + NY * NC]
    span = refs[NZ + NY * NC : NZ + 2 * NY * NC]
    o_ref = refs[NZ + 2 * NY * NC]
    q_all, k_all, v_all, part, chunks, stats = refs[NZ + 2 * NY * NC + 1 :]
    head = pl.program_id(0)
    zh, y, c = place[0], place[1], place[2]

    @pl.when(head == 0)
    def _():
        stats[...] = jnp.zeros_like(stats)

    for dz in range(NZ):
        q_all[dz * PAD : (dz + 1) * PAD, :] = qs[dz][...]
    for n in range(NY * NC):
        k_all[n * HKEYS : (n + 1) * HKEYS, :] = hist[n][0]
        v_all[n * HKEYS : (n + 1) * HKEYS, :] = hist[n][1]
        low = NHIST + n * PAD
        k_all[low : low + PAD, :] = span[n][0]
        v_all[low : low + PAD, :] = span[n][1]
    score = lax.dot_general(
        q_all[...], k_all[...], (((1,), (1,)), ((), ())), preferred_element_type=F32
    )

    row = lax.broadcasted_iota(jnp.int32, (QROWS, 1), 0)
    q_zh = lax.rem(zh + NZ - row // PAD, NZ)
    q_token = (q_zh * NY * NC + y * NC + c) * OWN + lax.rem(row, PAD)
    col = lax.broadcasted_iota(jnp.int32, (1, NSPAN), 1)
    block = col // PAD
    inside = lax.rem(col, PAD)
    k_y = lax.rem(y + NY - block // NC, NY)
    k_c = jnp.where(lax.rem(block, NC) == 0, c, 1 - c)
    k_token = (zh * NY * NC + k_y * NC + k_c) * OWN + inside
    k_frame = jnp.where(inside < OWN, k_token // FRAME_LEN, TOKENS)
    allowed = q_token // FRAME_LEN >= k_frame

    s_hist = score[:, :NHIST]
    s_span = jnp.where(allowed, score[:, NHIST:], -1e30)
    top = jnp.maximum(
        jnp.max(s_hist, axis=1, keepdims=True), jnp.max(s_span, axis=1, keepdims=True)
    )
    w_hist = jnp.exp2((s_hist - top) * SCALE)
    w_span = jnp.exp2((s_span - top) * SCALE)
    total = jnp.sum(w_hist, axis=1, keepdims=True) + jnp.sum(w_span, axis=1, keepdims=True)
    summed = jnp.dot(
        w_hist.astype(BF16), v_all[:NHIST, :], preferred_element_type=F32
    ) + jnp.dot(w_span.astype(BF16), v_all[NHIST:, :], preferred_element_type=F32)
    part[...] = summed / total

    for dz in range(NZ):
        home_z = lax.rem(zh + NZ - dz, NZ)
        for g in range(NG):
            low = dz * PAD + g * HOME
            chunks[home_z * NG + g, pl.ds(head * HOME, HOME), :] = part[low : low + HOME, :]

    lse = top * SCALE + jnp.log2(total)
    high = lse.astype(BF16).astype(F32)
    middle = (lse - high).astype(BF16).astype(F32)
    low_term = lse - high - middle
    token = lax.rem(row, PAD)
    lane = lax.broadcasted_iota(jnp.int32, (QROWS, HEAD_DIM), 1)
    here = (lane == head * HOME + lax.rem(token, HOME)) & (token < OWN)
    to_chunk = lax.broadcasted_iota(jnp.int32, (NZ * NG, QROWS), 0)
    from_row = lax.broadcasted_iota(jnp.int32, (NZ * NG, QROWS), 1)
    from_z = lax.rem(zh + NZ - from_row // PAD, NZ)
    pick = (to_chunk == from_z * NG + lax.rem(from_row, PAD) // HOME).astype(F32).astype(BF16)
    for n, term in enumerate((high, middle, low_term)):
        spread = jnp.where(here, term, 0.0).astype(BF16)
        stats[n] += jnp.dot(pick, spread, preferred_element_type=F32)

    @pl.when(head == HERE - 1)
    def _():
        for n in range(3):
            for chunk in range(NZ * NG):
                chunks[chunk, ROWS + n : ROWS + n + 1, :] = stats[n, chunk : chunk + 1, :]
        o_ref[...] = chunks[...].astype(BF16)


def attend(place, qs, hist, span):
    q_spec = pl.BlockSpec((PAD, HEAD_DIM), lambda h, p: (0, h))
    hist_spec = pl.BlockSpec((2, HKEYS, HEAD_DIM), lambda h, p: (0, 0, h))
    span_spec = pl.BlockSpec((2, PAD, HEAD_DIM), lambda h, p: (0, 0, h))
    keys = NHIST + NSPAN
    return pl.pallas_call(
        attend_kernel,
        out_shape=jax.ShapeDtypeStruct((NZ * NG, CHUNK, HEAD_DIM), BF16),
        grid_spec=pltpu.PrefetchScalarGridSpec(
            num_scalar_prefetch=1,
            grid=(HERE,),
            in_specs=[q_spec] * NZ + [hist_spec] * (NY * NC) + [span_spec] * (NY * NC),
            out_specs=pl.BlockSpec((NZ * NG, CHUNK, HEAD_DIM), lambda h, p: (0, 0, 0)),
            scratch_shapes=[
                pltpu.VMEM((QROWS, HEAD_DIM), BF16),
                pltpu.VMEM((keys, HEAD_DIM), BF16),
                pltpu.VMEM((keys, HEAD_DIM), BF16),
                pltpu.VMEM((QROWS, HEAD_DIM), F32),
                pltpu.VMEM((NZ * NG, CHUNK, HEAD_DIM), F32),
                pltpu.VMEM((3, NZ * NG, HEAD_DIM), F32),
            ],
        ),
        compiler_params=params(),
        cost_estimate=pl.CostEstimate(
            flops=4 * QROWS * keys * WIDE,
            bytes_accessed=4 * keys * WIDE,
            transcendentals=QROWS * keys * HERE,
        ),
    )(place, *qs, *hist, *span)


def merge_kernel(x_ref, o_ref, rows):
    eye = lax.broadcasted_iota(jnp.int32, (CHUNK, HEAD_DIM), 0) == lax.broadcasted_iota(
        jnp.int32, (CHUNK, HEAD_DIM), 1
    )
    for g in range(NG):
        parts = [x_ref[z * NG + g].astype(F32) for z in range(NZ)]
        lses = [
            (p[ROWS : ROWS + 1] + p[ROWS + 1 : ROWS + 2]) + p[ROWS + 2 : ROWS + 3] for p in parts
        ]
        top = jnp.maximum(jnp.maximum(lses[0], lses[1]), jnp.maximum(lses[2], lses[3]))
        weights = [jnp.exp2(v - top) for v in lses]
        total = (weights[0] + weights[1]) + (weights[2] + weights[3])
        out = jnp.zeros((CHUNK, HEAD_DIM), F32)
        for p, w in zip(parts, weights):
            share = jnp.sum(jnp.where(eye, w / total, 0.0), axis=1, keepdims=True)
            out = out + share * p
        rows[g] = out
        for e in range(HERE):
            low = (g * HERE + e) * HEAD_DIM
            o_ref[:, low : low + HEAD_DIM] = rows[g, e * HOME : (e + 1) * HOME, :].astype(BF16)


def merge(x):
    return pl.pallas_call(
        merge_kernel,
        out_shape=jax.ShapeDtypeStruct((HOME, HEADS * HEAD_DIM), BF16),
        in_specs=in_vmem(1),
        out_specs=pl.BlockSpec(memory_space=pltpu.VMEM),
        scratch_shapes=[pltpu.VMEM((NG, CHUNK, HEAD_DIM), F32)],
        compiler_params=params(),
    )(x)


def from_back(x, axis, size, back):
    return lax.ppermute(x, axis, [(i, (i + back) % size) for i in range(size)])


def on_device(span_qkv, history_kv):
    place = jnp.stack([lax.axis_index(a) for a in FRAMES]).astype(jnp.int32)
    hist_y = [history_kv] + [from_back(history_kv, "y", NY, d) for d in (1, 2, 3)]
    hist = []
    for block in hist_y:
        hist += [block, from_back(block, "c", NC, 1)]
    local = lax.all_to_all(pack(span_qkv), GROUPS, split_axis=0, concat_axis=0, tiled=True)
    q, kv = unpack(local)
    qs = [q] + [from_back(q, "zh", NZ, d) for d in (1, 2, 3)]
    span_y = [kv] + [from_back(kv, "y", NY, d) for d in (1, 2, 3)]
    span = []
    for block in span_y:
        span += [block, from_back(block, "c", NC, 1)]
    partial = attend(place, qs, hist, span)
    home = lax.all_to_all(partial, ("zh",) + GROUPS, split_axis=0, concat_axis=0, tiled=True)
    return merge(home)


def solution(mesh):
    cut = Mesh(mesh.devices.reshape(NZ, NY, NC, 2, 4), FRAMES + GROUPS)
    in_specs = (P(None, FRAMES + GROUPS, None), P(None, FRAMES, GROUPS))
    out_specs = P(FRAMES + GROUPS, None)
    return jax.shard_map(
        on_device, mesh=cut, in_specs=in_specs, out_specs=out_specs, check_vma=False
    )
```

```python
import math

import jax
import jax.numpy as jnp
from jax import lax
from jax.experimental import pallas as pl
from jax.experimental.pallas import tpu as pltpu
from jax.sharding import Mesh, PartitionSpec as P

HEADS = 40
HEAD_DIM = 128
TOKENS = 2304
HIST = 6144
FRAME_LEN = 768

FRAMES = ("zh", "y", "c")
GROUPS = ("zl", "x")
NZ, NY, NC, NG = 4, 4, 2, 8
HERE = HEADS // NG
WIDE = HERE * HEAD_DIM
HOME = TOKENS // (NZ * NY * NC * NG)
OWN = HOME * NG
HKEYS = HIST // (NZ * NY * NC)
NHIST = NY * NC * HKEYS
ROWS = HERE * HOME
CHUNK = 48
KV_CHUNK = 96
CHUNKS = NZ * NG
QROWS = CHUNKS * HOME
SKEYS = NY * NG * HOME
PIECES = 10
SCALE = math.log2(math.e) / math.sqrt(HEAD_DIM)
F32, BF16 = jnp.float32, jnp.bfloat16


def params(mib):
    return pltpu.CompilerParams(vmem_limit_bytes=mib * 2**20)


IN_VMEM = pl.BlockSpec(memory_space=pltpu.VMEM)
IN_SMEM = pl.BlockSpec(memory_space=pltpu.SMEM)
ANYWHERE = pl.BlockSpec(memory_space=pl.ANY)


def pack_kernel(x_ref, q_ref, kv_ref, q_rows, kv_rows):
    for g in range(NG):
        q_rows[g, ROWS:, :] = jnp.zeros((CHUNK - ROWS, HEAD_DIM), F32)
        kv_rows[g, 2 * ROWS :, :] = jnp.zeros((KV_CHUNK - 2 * ROWS, HEAD_DIM), F32)
        for e in range(HERE):
            cols = slice((g * HERE + e) * HEAD_DIM, (g * HERE + e + 1) * HEAD_DIM)
            low = e * HOME
            q_rows[g, low : low + HOME, :] = x_ref[0, :, cols].astype(F32)
            kv_rows[g, low : low + HOME, :] = x_ref[1, :, cols].astype(F32)
            low += ROWS
            kv_rows[g, low : low + HOME, :] = x_ref[2, :, cols].astype(F32)
        q = q_rows[g].astype(BF16)
        for z in range(NZ):
            q_ref[z * NG + g] = q
        kv_ref[g] = kv_rows[g].astype(BF16)


def pack(x):
    return pl.pallas_call(
        pack_kernel,
        out_shape=(
            jax.ShapeDtypeStruct((NZ * NG, CHUNK, HEAD_DIM), BF16),
            jax.ShapeDtypeStruct((NG, KV_CHUNK, HEAD_DIM), BF16),
        ),
        in_specs=[IN_VMEM],
        out_specs=(IN_VMEM, IN_VMEM),
        scratch_shapes=[
            pltpu.VMEM((NG, CHUNK, HEAD_DIM), F32),
            pltpu.VMEM((NG, KV_CHUNK, HEAD_DIM), F32),
        ],
        compiler_params=params(8),
    )(x)


def after_kernel(x_ref, *refs):
    refs[-1][...] = x_ref[...]


def after(x, *others):
    return pl.pallas_call(
        after_kernel,
        out_shape=jax.ShapeDtypeStruct(x.shape, x.dtype),
        in_specs=[IN_VMEM] + [ANYWHERE] * len(others),
        out_specs=IN_VMEM,
        compiler_params=params(8),
    )(x, *others)


def sort_kernel(*refs):
    o_ref, chunks, rows, sems = refs[-4:]
    copies = []
    for n in range(NY):
        where = chunks.at[pl.ds(n * NG, NG)]
        copies.append(pltpu.make_async_copy(refs[n], where, sems.at[n]))
    for copy in copies:
        copy.start()
    for copy in copies:
        copy.wait()
    rows[...] = chunks[...].astype(F32).reshape(CHUNKS * KV_CHUNK, HEAD_DIM)
    for i in range(2):
        for e in range(HERE):
            for t in range(HOME):
                row = (i * HERE + e) * HOME + t
                o_ref[i, e, t * CHUNKS : (t + 1) * CHUNKS, :] = rows[
                    pl.ds(row, CHUNKS, stride=KV_CHUNK), :
                ].astype(BF16)


def sort_span(span, *after):
    return pl.pallas_call(
        sort_kernel,
        out_shape=jax.ShapeDtypeStruct((2, HERE, SKEYS, HEAD_DIM), BF16),
        in_specs=[ANYWHERE] * (NY + len(after)),
        out_specs=IN_VMEM,
        scratch_shapes=[
            pltpu.VMEM((CHUNKS, KV_CHUNK, HEAD_DIM), BF16),
            pltpu.VMEM((CHUNKS * KV_CHUNK, HEAD_DIM), F32),
            pltpu.SemaphoreType.DMA((NY,)),
        ],
        compiler_params=params(8),
        cost_estimate=pl.CostEstimate(flops=0, bytes_accessed=0, transcendentals=0),
    )(*span, *after)


def sort_queries_kernel(x_ref, o_ref, rows):
    rows[...] = x_ref[...].astype(F32).reshape(CHUNKS * CHUNK, HEAD_DIM)
    for e in range(HERE):
        for t in range(HOME):
            row = e * HOME + t
            o_ref[e, t * CHUNKS : (t + 1) * CHUNKS, :] = rows[
                pl.ds(row, CHUNKS, stride=CHUNK), :
            ].astype(BF16)


def sort_queries(x):
    return pl.pallas_call(
        sort_queries_kernel,
        out_shape=jax.ShapeDtypeStruct((HERE, QROWS, HEAD_DIM), BF16),
        in_specs=[IN_VMEM],
        out_specs=IN_VMEM,
        scratch_shapes=[pltpu.VMEM((CHUNKS * CHUNK, HEAD_DIM), F32)],
        compiler_params=params(8),
    )(x)


def keys_and_values(refs):
    whole = [(refs[n].at[0], refs[n].at[1]) for n in range(6)]
    return whole + [(refs[6], refs[8]), (refs[7], refs[9])]


def against(queries, keys):
    return lax.dot_general(
        queries, keys, (((1,), (1,)), ((), ())), preferred_element_type=F32
    )


def attend_kernel(place, q_ref, own_span, other_span, *refs):
    hist = keys_and_values(refs[:PIECES])
    o_ref, q_all, rows, kv_span, k_hist, v_hist, sums, tops, totals = refs[PIECES : PIECES + 9]
    q_sem, span_sems, sems = refs[PIECES + 9 :]
    zh, y, c = place[0], place[1], place[2]
    early, late = [], []
    early.append(pltpu.make_async_copy(q_ref, q_all, q_sem.at[0]))
    for b, source in enumerate((own_span, other_span)):
        where = kv_span.at[:, :, pl.ds(b * SKEYS, SKEYS)]
        early.append(pltpu.make_async_copy(source, where, span_sems.at[b]))
    for n, (keys, values) in enumerate(hist):
        where = pl.ds(n * HKEYS, HKEYS)
        late.append(pltpu.make_async_copy(keys, k_hist.at[where], sems.at[0, n]))
        late.append(pltpu.make_async_copy(values, v_hist.at[where], sems.at[1, n]))
    for copy in early + late:
        copy.start()

    row = lax.broadcasted_iota(jnp.int32, (QROWS, 1), 0)
    sender = lax.rem(row, CHUNKS)
    index = ((sender // NG) * NY + y) * NC + c
    q_token = index * OWN + lax.rem(sender, NG) * HOME + row // CHUNKS
    q_frame = q_token // FRAME_LEN
    col = lax.broadcasted_iota(jnp.int32, (1, NC * SKEYS), 1)
    core = jnp.where(col < SKEYS, c, 1 - c)
    col = lax.rem(col, SKEYS)
    sender = lax.rem(col, CHUNKS)
    index = (zh * NY + lax.rem(y + NY - sender // NG, NY)) * NC + core
    k_token = index * OWN + lax.rem(sender, NG) * HOME + col // CHUNKS
    allowed = q_frame >= k_token // FRAME_LEN

    for copy in early:
        copy.wait()
    for e in range(HERE):
        score = jnp.where(allowed, against(q_all[e], kv_span[0, e]), -1e30)
        top = jnp.max(score, axis=1, keepdims=True)
        weight = jnp.exp2((score - top) * SCALE)
        tops[e] = jnp.broadcast_to(top, (QROWS, HEAD_DIM))
        totals[e] = jnp.broadcast_to(
            jnp.sum(weight, axis=1, keepdims=True), (QROWS, HEAD_DIM)
        )
        sums[e] = jnp.dot(weight.astype(BF16), kv_span[1, e], preferred_element_type=F32)
    for copy in late:
        copy.wait()
    lane = lax.broadcasted_iota(jnp.int32, (CHUNKS, HEAD_DIM), 1)
    lses = jnp.zeros((CHUNKS, HEAD_DIM), F32)
    for e in range(HERE):
        cols = slice(e * HEAD_DIM, (e + 1) * HEAD_DIM)
        score = against(q_all[e], k_hist[:, cols])
        before = tops[e]
        top = jnp.maximum(before, jnp.max(score, axis=1, keepdims=True))
        factor = jnp.exp2((before - top) * SCALE)
        weight = jnp.exp2((score - top[:, :1]) * SCALE)
        total = totals[e] * factor + jnp.sum(weight, axis=1, keepdims=True)
        summed = sums[e] * factor + jnp.dot(
            weight.astype(BF16), v_hist[:, cols], preferred_element_type=F32
        )
        partial = summed / total
        lse = top * SCALE + jnp.log2(total)
        for t in range(HOME):
            here = slice(t * CHUNKS, (t + 1) * CHUNKS)
            row = e * HOME + t
            rows[pl.ds(row, CHUNKS, stride=CHUNK), :] = partial[here]
            lses = jnp.where(lane == row, lse[here], lses)

    high = lses.astype(BF16).astype(F32)
    middle = (lses - high).astype(BF16).astype(F32)
    for n, term in enumerate((high, middle, lses - high - middle)):
        rows[pl.ds(ROWS + n, CHUNKS, stride=CHUNK), :] = term
    o_ref[...] = rows[...].reshape(CHUNKS, CHUNK, HEAD_DIM).astype(BF16)


def attend(place, q, own_span, other_span, hist):
    keys = NHIST + NC * SKEYS
    by_head = pltpu.VMEM((HERE, QROWS, HEAD_DIM), F32)
    return pl.pallas_call(
        attend_kernel,
        out_shape=jax.ShapeDtypeStruct((CHUNKS, CHUNK, HEAD_DIM), BF16),
        in_specs=[IN_SMEM] + [ANYWHERE] * (3 + PIECES),
        out_specs=IN_VMEM,
        scratch_shapes=[
            pltpu.VMEM((HERE, QROWS, HEAD_DIM), BF16),
            pltpu.VMEM((CHUNKS * CHUNK, HEAD_DIM), F32),
            pltpu.VMEM((2, HERE, NC * SKEYS, HEAD_DIM), BF16),
            pltpu.VMEM((NHIST, WIDE), BF16),
            pltpu.VMEM((NHIST, WIDE), BF16),
            by_head,
            by_head,
            by_head,
            pltpu.SemaphoreType.DMA((1,)),
            pltpu.SemaphoreType.DMA((NC,)),
            pltpu.SemaphoreType.DMA((2, NY * NC)),
        ],
        compiler_params=params(24),
        cost_estimate=pl.CostEstimate(
            flops=4 * QROWS * keys * WIDE,
            bytes_accessed=4 * keys * WIDE,
            transcendentals=QROWS * keys * HERE,
        ),
    )(place, q, own_span, other_span, *hist)


def merge_kernel(x_ref, o_ref, rows):
    eye = lax.broadcasted_iota(jnp.int32, (CHUNK, HEAD_DIM), 0) == lax.broadcasted_iota(
        jnp.int32, (CHUNK, HEAD_DIM), 1
    )
    for g in range(NG):
        parts = [x_ref[z * NG + g].astype(F32) for z in range(NZ)]
        lses = [
            (p[ROWS : ROWS + 1] + p[ROWS + 1 : ROWS + 2]) + p[ROWS + 2 : ROWS + 3] for p in parts
        ]
        top = jnp.maximum(jnp.maximum(lses[0], lses[1]), jnp.maximum(lses[2], lses[3]))
        weights = [jnp.exp2(v - top) for v in lses]
        total = (weights[0] + weights[1]) + (weights[2] + weights[3])
        out = jnp.zeros((CHUNK, HEAD_DIM), F32)
        for p, w in zip(parts, weights):
            share = jnp.sum(jnp.where(eye, w / total, 0.0), axis=1, keepdims=True)
            out = out + share * p
        rows[g] = out
        for e in range(HERE):
            low = (g * HERE + e) * HEAD_DIM
            o_ref[:, low : low + HEAD_DIM] = rows[g, e * HOME : (e + 1) * HOME, :].astype(BF16)


def merge(x):
    return pl.pallas_call(
        merge_kernel,
        out_shape=jax.ShapeDtypeStruct((HOME, HEADS * HEAD_DIM), BF16),
        in_specs=[IN_VMEM],
        out_specs=IN_VMEM,
        scratch_shapes=[pltpu.VMEM((NG, CHUNK, HEAD_DIM), F32)],
        compiler_params=params(8),
    )(x)


def from_back(x, axis, size, back):
    return lax.ppermute(x, axis, [(i, (i + back) % size) for i in range(size)])


def exchange(x, axes):
    return lax.all_to_all(x, axes, split_axis=0, concat_axis=0, tiled=True)


def on_device(span_qkv, history_kv):
    place = jnp.stack([lax.axis_index(a) for a in FRAMES]).astype(jnp.int32)
    other = lambda x: from_back(x, "c", NC, 1)
    back = from_back(history_kv, "y", NY, 1)
    ahead = from_back(history_kv, "y", NY, NY - 1)
    near = [history_kv, other(history_kv), back, other(back), ahead, other(ahead)]
    keys = from_back(back[0], "y", NY, 1)
    values = from_back(ahead[1], "y", NY, NY - 1)
    hist = near + [keys, other(keys), values, other(values)]

    q, kv = pack(span_qkv)
    kv = after(exchange(kv, GROUPS), back, ahead)
    q = exchange(q, ("zh",) + GROUPS)
    span = sort_span([kv] + [from_back(kv, "y", NY, d) for d in range(1, NY)], keys, values)
    partial = attend(place, sort_queries(q), span, other(span), hist)
    return merge(exchange(partial, ("zh",) + GROUPS))


def solution(mesh):
    cut = Mesh(mesh.devices.reshape(NZ, NY, NC, 2, 4), FRAMES + GROUPS)
    in_specs = (P(None, FRAMES + GROUPS, None), P(None, FRAMES, GROUPS))
    out_specs = P(FRAMES + GROUPS, None)
    return jax.shard_map(
        on_device, mesh=cut, in_specs=in_specs, out_specs=out_specs, check_vma=False
    )
```

```python
import math

import jax
import jax.numpy as jnp
from jax import lax
from jax.experimental import pallas as pl
from jax.experimental.pallas import tpu as pltpu
from jax.sharding import Mesh, PartitionSpec as P

HEADS = 40
HEAD_DIM = 128
TOKENS = 2304
HIST = 6144
FRAME_LEN = 768

FRAMES = ("zh", "y", "c")
GROUPS = ("zl", "x")
PLANE = ("zh", "x", "zl")
NX, NZL = 4, 2
NZ, NY, NC, NG = 4, 4, 2, 8
HERE = HEADS // NG
WIDE = HERE * HEAD_DIM
HOME = TOKENS // (NZ * NY * NC * NG)
OWN = HOME * NG
HKEYS = HIST // (NZ * NY * NC)
NHIST = NY * NC * HKEYS
ROWS = HERE * HOME
CHUNK = 48
KV_CHUNK = 96
CHUNKS = NZ * NG
QROWS = CHUNKS * HOME
SKEYS = NY * NG * HOME
KEYS = NHIST + NC * SKEYS
PIECES = 10
HEAD_PARTS = ((0, 2), (2, 5))
SCALE = math.log2(math.e) / math.sqrt(HEAD_DIM)
F32, BF16 = jnp.float32, jnp.bfloat16


def params(mib):
    return pltpu.CompilerParams(vmem_limit_bytes=mib * 2**20)


IN_VMEM = pl.BlockSpec(memory_space=pltpu.VMEM)
IN_SMEM = pl.BlockSpec(memory_space=pltpu.SMEM)
IN_HBM = pl.BlockSpec(memory_space=pltpu.HBM)
ANYWHERE = pl.BlockSpec(memory_space=pl.ANY)


def group_of(m):
    return (m % NZL) * NX + m // NZL


def pack_kernel(x_ref, q_ref, kv_ref, q_rows, kv_rows):
    for g in range(NG):
        q_rows[g, ROWS:, :] = jnp.zeros((CHUNK - ROWS, HEAD_DIM), F32)
        kv_rows[g, 2 * ROWS :, :] = jnp.zeros((KV_CHUNK - 2 * ROWS, HEAD_DIM), F32)
        for e in range(HERE):
            cols = slice((g * HERE + e) * HEAD_DIM, (g * HERE + e + 1) * HEAD_DIM)
            low = e * HOME
            q_rows[g, low : low + HOME, :] = x_ref[0, :, cols].astype(F32)
            kv_rows[g, low : low + HOME, :] = x_ref[1, :, cols].astype(F32)
            low += ROWS
            kv_rows[g, low : low + HOME, :] = x_ref[2, :, cols].astype(F32)
        q = q_rows[g].astype(BF16)
        member = (g % NX) * NZL + g // NX
        for z in range(NZ):
            q_ref[z * NG + member] = q
        kv_ref[g] = kv_rows[g].astype(BF16)


def pack(x):
    return pl.pallas_call(
        pack_kernel,
        out_shape=(
            jax.ShapeDtypeStruct((NZ * NG, CHUNK, HEAD_DIM), BF16),
            jax.ShapeDtypeStruct((NG, KV_CHUNK, HEAD_DIM), BF16),
        ),
        in_specs=[IN_VMEM],
        out_specs=(IN_VMEM, IN_VMEM),
        scratch_shapes=[
            pltpu.VMEM((NG, CHUNK, HEAD_DIM), F32),
            pltpu.VMEM((NG, KV_CHUNK, HEAD_DIM), F32),
        ],
        compiler_params=params(8),
    )(x)


def after_kernel(x_ref, *refs):
    refs[-1][...] = x_ref[...]


def after(x, *others):
    return pl.pallas_call(
        after_kernel,
        out_shape=jax.ShapeDtypeStruct(x.shape, x.dtype),
        in_specs=[IN_VMEM] + [ANYWHERE] * len(others),
        out_specs=IN_VMEM,
        compiler_params=params(8),
    )(x, *others)


def sort_kernel(*refs):
    o_ref, chunks, rows, sems = refs[-4:]
    copies = []
    for n in range(NY):
        where = chunks.at[pl.ds(n * NG, NG)]
        copies.append(pltpu.make_async_copy(refs[n], where, sems.at[n]))
    for copy in copies:
        copy.start()
    for copy in copies:
        copy.wait()
    rows[...] = chunks[...].astype(F32).reshape(CHUNKS * KV_CHUNK, HEAD_DIM)
    for i in range(2):
        for e in range(HERE):
            for t in range(HOME):
                row = (i * HERE + e) * HOME + t
                o_ref[i, t * CHUNKS : (t + 1) * CHUNKS, e * HEAD_DIM : (e + 1) * HEAD_DIM] = rows[
                    pl.ds(row, CHUNKS, stride=KV_CHUNK), :
                ].astype(BF16)


def sort_span(span, *after):
    return pl.pallas_call(
        sort_kernel,
        out_shape=jax.ShapeDtypeStruct((2, SKEYS, WIDE), BF16),
        in_specs=[ANYWHERE] * (NY + len(after)),
        out_specs=IN_VMEM,
        scratch_shapes=[
            pltpu.VMEM((CHUNKS, KV_CHUNK, HEAD_DIM), BF16),
            pltpu.VMEM((CHUNKS * KV_CHUNK, HEAD_DIM), F32),
            pltpu.SemaphoreType.DMA((NY,)),
        ],
        compiler_params=params(8),
        cost_estimate=pl.CostEstimate(flops=0, bytes_accessed=0, transcendentals=0),
    )(*span, *after)


def against(queries, keys):
    return lax.dot_general(
        queries, keys, (((1,), (1,)), ((), ())), preferred_element_type=F32
    )


def attend_kernel(place, q_ref, *refs):
    o_ref, kv_all, q_all, rows, sems = refs[PIECES + NC :]
    k_ref, v_ref = kv_all.at[0], kv_all.at[1]
    copies = []
    for n, (low, high) in enumerate(HEAD_PARTS):
        cols = pl.ds(low * HEAD_DIM, (high - low) * HEAD_DIM)
        moves = []
        for m in range(6):
            moves.append((refs[m].at[:, :, cols], kv_all.at[:, pl.ds(m * HKEYS, HKEYS), cols]))
        for m in range(2):
            where = pl.ds((6 + m) * HKEYS, HKEYS)
            moves.append((refs[6 + m].at[:, cols], k_ref.at[where, cols]))
            moves.append((refs[8 + m].at[:, cols], v_ref.at[where, cols]))
        for b in range(NC):
            where = pl.ds(NHIST + b * SKEYS, SKEYS)
            moves.append((refs[PIECES + b].at[:, :, cols], kv_all.at[:, where, cols]))
        copies.append(
            [pltpu.make_async_copy(x, to, sems.at[n, m]) for m, (x, to) in enumerate(moves)]
        )
        for copy in copies[n]:
            copy.start()
    rows[...] = q_ref[...].astype(F32).reshape(CHUNKS * CHUNK, HEAD_DIM)
    for e in range(HERE):
        for t in range(HOME):
            row = e * HOME + t
            q_all[e, t * CHUNKS : (t + 1) * CHUNKS, :] = rows[
                pl.ds(row, CHUNKS, stride=CHUNK), :
            ].astype(BF16)

    zh, y, c = place[0], place[1], place[2]
    row = lax.broadcasted_iota(jnp.int32, (QROWS, 1), 0)
    sender = lax.rem(row, CHUNKS)
    index = ((sender // NG) * NY + y) * NC + c
    member = lax.rem(sender, NG)
    group = lax.rem(member, NZL) * NX + member // NZL
    q_token = index * OWN + group * HOME + row // CHUNKS
    q_frame = q_token // FRAME_LEN
    col = lax.broadcasted_iota(jnp.int32, (1, NC * SKEYS), 1)
    core = jnp.where(col < SKEYS, c, 1 - c)
    col = lax.rem(col, SKEYS)
    sender = lax.rem(col, CHUNKS)
    index = (zh * NY + lax.rem(y + NY - sender // NG, NY)) * NC + core
    k_token = index * OWN + lax.rem(sender, NG) * HOME + col // CHUNKS
    k_frame = k_token // FRAME_LEN

    lane = lax.broadcasted_iota(jnp.int32, (CHUNKS, HEAD_DIM), 1)
    lses = jnp.zeros((CHUNKS, HEAD_DIM), F32)
    starts = {low: copies[n] for n, (low, high) in enumerate(HEAD_PARTS)}
    upcoming = None
    for e in range(HERE):
        for copy in starts.get(e, []) if e == 0 else []:
            copy.wait()
        score = against(q_all[0], k_ref[:, :HEAD_DIM]) if e == 0 else upcoming
        for copy in starts.get(e + 1, []):
            copy.wait()
        if e + 1 < HERE:
            upcoming = against(q_all[e + 1], k_ref[:, (e + 1) * HEAD_DIM : (e + 2) * HEAD_DIM])
        s_hist = score[:, :NHIST]
        s_span = jnp.where(q_frame >= k_frame, score[:, NHIST:], -1e30)
        top = jnp.maximum(
            jnp.max(s_hist, axis=1, keepdims=True), jnp.max(s_span, axis=1, keepdims=True)
        )
        weight = jnp.exp2((jnp.concatenate([s_hist, s_span], axis=1) - top) * SCALE)
        total = jnp.sum(weight, axis=1, keepdims=True)
        values = v_ref[:, e * HEAD_DIM : (e + 1) * HEAD_DIM]
        summed = jnp.dot(weight.astype(BF16), values, preferred_element_type=F32)
        partial = summed / total
        lse = top * SCALE + jnp.log2(total)
        for t in range(HOME):
            here = slice(t * CHUNKS, (t + 1) * CHUNKS)
            row = e * HOME + t
            rows[pl.ds(row, CHUNKS, stride=CHUNK), :] = partial[here]
            lses = jnp.where(lane == row, lse[here], lses)

    high = lses.astype(BF16).astype(F32)
    middle = (lses - high).astype(BF16).astype(F32)
    for n, term in enumerate((high, middle, lses - high - middle)):
        rows[pl.ds(ROWS + n, CHUNKS, stride=CHUNK), :] = term
    o_ref[...] = rows[...].reshape(CHUNKS, CHUNK, HEAD_DIM).astype(BF16)


def attend(place, q, hist, spans):
    return pl.pallas_call(
        attend_kernel,
        out_shape=jax.ShapeDtypeStruct((CHUNKS, CHUNK, HEAD_DIM), BF16),
        in_specs=[IN_SMEM, IN_VMEM] + [ANYWHERE] * (PIECES + NC),
        out_specs=IN_VMEM,
        scratch_shapes=[
            pltpu.VMEM((2, KEYS, WIDE), BF16),
            pltpu.VMEM((HERE, QROWS, HEAD_DIM), BF16),
            pltpu.VMEM((CHUNKS * CHUNK, HEAD_DIM), F32),
            pltpu.SemaphoreType.DMA((len(HEAD_PARTS), PIECES + NC)),
        ],
        compiler_params=params(24),
        cost_estimate=pl.CostEstimate(
            flops=4 * QROWS * KEYS * WIDE,
            bytes_accessed=4 * KEYS * WIDE,
            transcendentals=QROWS * KEYS * HERE,
        ),
    )(place, q, *hist, *spans)


def merge_kernel(x_ref, o_ref, rows):
    eye = lax.broadcasted_iota(jnp.int32, (CHUNK, HEAD_DIM), 0) == lax.broadcasted_iota(
        jnp.int32, (CHUNK, HEAD_DIM), 1
    )
    for m in range(NG):
        g = group_of(m)
        parts = [x_ref[z * NG + m].astype(F32) for z in range(NZ)]
        lses = [
            (p[ROWS : ROWS + 1] + p[ROWS + 1 : ROWS + 2]) + p[ROWS + 2 : ROWS + 3] for p in parts
        ]
        top = jnp.maximum(jnp.maximum(lses[0], lses[1]), jnp.maximum(lses[2], lses[3]))
        weights = [jnp.exp2(v - top) for v in lses]
        total = (weights[0] + weights[1]) + (weights[2] + weights[3])
        out = jnp.zeros((CHUNK, HEAD_DIM), F32)
        for p, w in zip(parts, weights):
            share = jnp.sum(jnp.where(eye, w / total, 0.0), axis=1, keepdims=True)
            out = out + share * p
        rows[g] = out
        for e in range(HERE):
            low = (g * HERE + e) * HEAD_DIM
            o_ref[:, low : low + HEAD_DIM] = rows[g, e * HOME : (e + 1) * HOME, :].astype(BF16)


def merge(x):
    return pl.pallas_call(
        merge_kernel,
        out_shape=jax.ShapeDtypeStruct((HOME, HEADS * HEAD_DIM), BF16),
        in_specs=[IN_VMEM],
        out_specs=IN_VMEM,
        scratch_shapes=[pltpu.VMEM((NG, CHUNK, HEAD_DIM), F32)],
        compiler_params=params(8),
    )(x)


def from_back(x, axis, size, back):
    return lax.ppermute(x, axis, [(i, (i + back) % size) for i in range(size)])


def exchange(x, axes):
    return lax.all_to_all(x, axes, split_axis=0, concat_axis=0, tiled=True)


def on_device(span_qkv, history_kv):
    place = jnp.stack([lax.axis_index(a) for a in FRAMES]).astype(jnp.int32)
    other = lambda x: from_back(x, "c", NC, 1)
    back = from_back(history_kv, "y", NY, 1)
    ahead = from_back(history_kv, "y", NY, NY - 1)
    near = [history_kv, other(history_kv), back, other(back), ahead, other(ahead)]
    keys = from_back(back[0], "y", NY, 1)
    values = from_back(ahead[1], "y", NY, NY - 1)
    hist = near + [keys, other(keys), values, other(values)]

    q, kv = pack(span_qkv)
    kv = after(exchange(kv, GROUPS), back, ahead)
    q = exchange(q, PLANE)
    span = sort_span([kv] + [from_back(kv, "y", NY, d) for d in range(1, NY)], keys, values)
    partial = attend(place, q, hist, [span, other(span)])
    return merge(exchange(partial, PLANE))


def solution(mesh):
    cut = Mesh(mesh.devices.reshape(NZ, NY, NC, 2, 4), FRAMES + GROUPS)
    in_specs = (P(None, FRAMES + GROUPS, None), P(None, FRAMES, GROUPS))
    out_specs = P(FRAMES + GROUPS, None)
    return jax.shard_map(
        on_device, mesh=cut, in_specs=in_specs, out_specs=out_specs, check_vma=False
    )
```

```python
import math

import jax
import jax.numpy as jnp
from jax import lax
from jax.experimental import pallas as pl
from jax.experimental.pallas import tpu as pltpu
from jax.sharding import Mesh, PartitionSpec as P

HEADS = 40
HEAD_DIM = 128
TOKENS = 2304
HIST = 6144
FRAME_LEN = 768

FRAMES = ("zh", "y", "c")
GROUPS = ("zl", "x")
PLANE = ("zh", "x", "zl")
NX, NZL = 4, 2
NZ, NY, NC, NG = 4, 4, 2, 8
HERE = HEADS // NG
WIDE = HERE * HEAD_DIM
HOME = TOKENS // (NZ * NY * NC * NG)
OWN = HOME * NG
HKEYS = HIST // (NZ * NY * NC)
NHIST = NY * NC * HKEYS
ROWS = HERE * HOME
CHUNK = 48
KV_CHUNK = 96
CHUNKS = NZ * NG
QROWS = CHUNKS * HOME
SKEYS = NY * NG * HOME
KEYS = NHIST + NC * SKEYS
PIECES = 10
HEAD_PARTS = ((0, 2), (2, 5))
SCALE = math.log2(math.e) / math.sqrt(HEAD_DIM)
F32, BF16 = jnp.float32, jnp.bfloat16


def params(mib):
    return pltpu.CompilerParams(vmem_limit_bytes=mib * 2**20)


IN_VMEM = pl.BlockSpec(memory_space=pltpu.VMEM)
IN_SMEM = pl.BlockSpec(memory_space=pltpu.SMEM)
IN_HBM = pl.BlockSpec(memory_space=pltpu.HBM)
ANYWHERE = pl.BlockSpec(memory_space=pl.ANY)


def group_of(m):
    return (m % NZL) * NX + m // NZL


def pack_kernel(x_ref, q_ref, kv_ref, q_rows, kv_rows):
    for g in range(NG):
        q_rows[g, ROWS:, :] = jnp.zeros((CHUNK - ROWS, HEAD_DIM), F32)
        kv_rows[g, 2 * ROWS :, :] = jnp.zeros((KV_CHUNK - 2 * ROWS, HEAD_DIM), F32)
        for e in range(HERE):
            cols = slice((g * HERE + e) * HEAD_DIM, (g * HERE + e + 1) * HEAD_DIM)
            low = e * HOME
            q_rows[g, low : low + HOME, :] = x_ref[0, :, cols].astype(F32)
            kv_rows[g, low : low + HOME, :] = x_ref[1, :, cols].astype(F32)
            low += ROWS
            kv_rows[g, low : low + HOME, :] = x_ref[2, :, cols].astype(F32)
        q = q_rows[g].astype(BF16)
        member = (g % NX) * NZL + g // NX
        for z in range(NZ):
            q_ref[z * NG + member] = q
        kv_ref[g] = kv_rows[g].astype(BF16)


def pack(x):
    return pl.pallas_call(
        pack_kernel,
        out_shape=(
            jax.ShapeDtypeStruct((NZ * NG, CHUNK, HEAD_DIM), BF16),
            jax.ShapeDtypeStruct((NG, KV_CHUNK, HEAD_DIM), BF16),
        ),
        in_specs=[IN_VMEM],
        out_specs=(IN_VMEM, IN_VMEM),
        scratch_shapes=[
            pltpu.VMEM((NG + 1, CHUNK, HEAD_DIM), F32),
            pltpu.VMEM((NG + 1, KV_CHUNK, HEAD_DIM), F32),
        ],
        compiler_params=params(8),
    )(x)


def after_kernel(x_ref, *refs):
    refs[-1][...] = x_ref[...]


def after(x, *others):
    return pl.pallas_call(
        after_kernel,
        out_shape=jax.ShapeDtypeStruct(x.shape, x.dtype),
        in_specs=[IN_VMEM] + [ANYWHERE] * len(others),
        out_specs=IN_VMEM,
        compiler_params=params(8),
    )(x, *others)


def sort_kernel(*refs):
    o_ref, chunks, rows, sems = refs[-4:]
    copies = []
    for n in range(NY):
        where = chunks.at[pl.ds(n * NG, NG)]
        copies.append(pltpu.make_async_copy(refs[n], where, sems.at[n]))
    for copy in copies:
        copy.start()
    for copy in copies:
        copy.wait()
    rows[: CHUNKS * KV_CHUNK, :] = (
        chunks[...].astype(F32).reshape(CHUNKS * KV_CHUNK, HEAD_DIM)
    )
    for i in range(2):
        for e in range(HERE):
            for t in range(HOME):
                row = (i * HERE + e) * HOME + t
                o_ref[i, t * CHUNKS : (t + 1) * CHUNKS, e * HEAD_DIM : (e + 1) * HEAD_DIM] = rows[
                    pl.ds(row, CHUNKS, stride=KV_CHUNK), :
                ].astype(BF16)


def sort_span(span, *after):
    return pl.pallas_call(
        sort_kernel,
        out_shape=jax.ShapeDtypeStruct((2, SKEYS, WIDE), BF16),
        in_specs=[ANYWHERE] * (NY + len(after)),
        out_specs=IN_VMEM,
        scratch_shapes=[
            pltpu.VMEM((CHUNKS, KV_CHUNK, HEAD_DIM), BF16),
            pltpu.VMEM(((CHUNKS + 1) * KV_CHUNK, HEAD_DIM), F32),
            pltpu.SemaphoreType.DMA((NY,)),
        ],
        compiler_params=params(8),
        cost_estimate=pl.CostEstimate(flops=0, bytes_accessed=0, transcendentals=0),
    )(*span, *after)


def against(queries, keys):
    return lax.dot_general(
        queries, keys, (((1,), (1,)), ((), ())), preferred_element_type=F32
    )


def attend_kernel(place, q_ref, *refs):
    o_ref, kv_all, q_all, rows, sems = refs[PIECES + NC :]
    k_ref, v_ref = kv_all.at[0], kv_all.at[1]
    copies = []
    for n, (low, high) in enumerate(HEAD_PARTS):
        cols = pl.ds(low * HEAD_DIM, (high - low) * HEAD_DIM)
        moves = []
        for m in range(6):
            moves.append((refs[m].at[:, :, cols], kv_all.at[:, pl.ds(m * HKEYS, HKEYS), cols]))
        for m in range(2):
            where = pl.ds((6 + m) * HKEYS, HKEYS)
            moves.append((refs[6 + m].at[:, cols], k_ref.at[where, cols]))
            moves.append((refs[8 + m].at[:, cols], v_ref.at[where, cols]))
        for b in range(NC):
            where = pl.ds(NHIST + b * SKEYS, SKEYS)
            moves.append((refs[PIECES + b].at[:, :, cols], kv_all.at[:, where, cols]))
        copies.append(
            [pltpu.make_async_copy(x, to, sems.at[n, m]) for m, (x, to) in enumerate(moves)]
        )
        for copy in copies[n]:
            copy.start()
    rows[: CHUNKS * CHUNK, :] = q_ref[...].astype(F32).reshape(CHUNKS * CHUNK, HEAD_DIM)
    for e in range(HERE):
        for t in range(HOME):
            row = e * HOME + t
            q_all[e, t * CHUNKS : (t + 1) * CHUNKS, :] = rows[
                pl.ds(row, CHUNKS, stride=CHUNK), :
            ].astype(BF16)

    zh, y, c = place[0], place[1], place[2]
    row = lax.broadcasted_iota(jnp.int32, (QROWS, 1), 0)
    sender = lax.rem(row, CHUNKS)
    index = ((sender // NG) * NY + y) * NC + c
    member = lax.rem(sender, NG)
    group = lax.rem(member, NZL) * NX + member // NZL
    q_token = index * OWN + group * HOME + row // CHUNKS
    q_frame = q_token // FRAME_LEN
    col = lax.broadcasted_iota(jnp.int32, (1, NC * SKEYS), 1)
    core = jnp.where(col < SKEYS, c, 1 - c)
    col = lax.rem(col, SKEYS)
    sender = lax.rem(col, CHUNKS)
    index = (zh * NY + lax.rem(y + NY - sender // NG, NY)) * NC + core
    k_token = index * OWN + lax.rem(sender, NG) * HOME + col // CHUNKS
    k_frame = k_token // FRAME_LEN

    lane = lax.broadcasted_iota(jnp.int32, (CHUNKS, HEAD_DIM), 1)
    lses = jnp.zeros((CHUNKS, HEAD_DIM), F32)
    starts = {low: copies[n] for n, (low, high) in enumerate(HEAD_PARTS)}
    upcoming = None
    for e in range(HERE):
        for copy in starts.get(e, []) if e == 0 else []:
            copy.wait()
        score = against(q_all[0], k_ref[:, :HEAD_DIM]) if e == 0 else upcoming
        for copy in starts.get(e + 1, []):
            copy.wait()
        if e + 1 < HERE:
            upcoming = against(q_all[e + 1], k_ref[:, (e + 1) * HEAD_DIM : (e + 2) * HEAD_DIM])
        s_hist = score[:, :NHIST]
        s_span = jnp.where(q_frame >= k_frame, score[:, NHIST:], -1e30)
        top = jnp.maximum(
            jnp.max(s_hist, axis=1, keepdims=True), jnp.max(s_span, axis=1, keepdims=True)
        )
        weight = jnp.exp2((jnp.concatenate([s_hist, s_span], axis=1) - top) * SCALE)
        total = jnp.sum(weight, axis=1, keepdims=True)
        values = v_ref[:, e * HEAD_DIM : (e + 1) * HEAD_DIM]
        summed = jnp.dot(weight.astype(BF16), values, preferred_element_type=F32)
        partial = summed / total
        lse = top * SCALE + jnp.log2(total)
        for t in range(HOME):
            here = slice(t * CHUNKS, (t + 1) * CHUNKS)
            row = e * HOME + t
            rows[pl.ds(row, CHUNKS, stride=CHUNK), :] = partial[here]
            lses = jnp.where(lane == row, lse[here], lses)

    high = lses.astype(BF16).astype(F32)
    middle = (lses - high).astype(BF16).astype(F32)
    for n, term in enumerate((high, middle, lses - high - middle)):
        rows[pl.ds(ROWS + n, CHUNKS, stride=CHUNK), :] = term
    chunks = rows[: CHUNKS * CHUNK, :].reshape(CHUNKS, CHUNK, HEAD_DIM)
    o_ref[...] = chunks.astype(BF16)


def attend(place, q, hist, spans):
    return pl.pallas_call(
        attend_kernel,
        out_shape=jax.ShapeDtypeStruct((CHUNKS, CHUNK, HEAD_DIM), BF16),
        in_specs=[IN_SMEM, IN_VMEM] + [ANYWHERE] * (PIECES + NC),
        out_specs=IN_VMEM,
        scratch_shapes=[
            pltpu.VMEM((2, KEYS, WIDE), BF16),
            pltpu.VMEM((HERE, QROWS, HEAD_DIM), BF16),
            pltpu.VMEM(((CHUNKS + 1) * CHUNK, HEAD_DIM), F32),
            pltpu.SemaphoreType.DMA((len(HEAD_PARTS), PIECES + NC)),
        ],
        compiler_params=params(24),
        cost_estimate=pl.CostEstimate(
            flops=4 * QROWS * KEYS * WIDE,
            bytes_accessed=4 * KEYS * WIDE,
            transcendentals=QROWS * KEYS * HERE,
        ),
    )(place, q, *hist, *spans)


def merge_kernel(x_ref, o_ref, rows):
    eye = lax.broadcasted_iota(jnp.int32, (CHUNK, HEAD_DIM), 0) == lax.broadcasted_iota(
        jnp.int32, (CHUNK, HEAD_DIM), 1
    )
    for m in range(NG):
        g = group_of(m)
        parts = [x_ref[z * NG + m].astype(F32) for z in range(NZ)]
        lses = [
            (p[ROWS : ROWS + 1] + p[ROWS + 1 : ROWS + 2]) + p[ROWS + 2 : ROWS + 3] for p in parts
        ]
        top = jnp.maximum(jnp.maximum(lses[0], lses[1]), jnp.maximum(lses[2], lses[3]))
        weights = [jnp.exp2(v - top) for v in lses]
        total = (weights[0] + weights[1]) + (weights[2] + weights[3])
        out = jnp.zeros((CHUNK, HEAD_DIM), F32)
        for p, w in zip(parts, weights):
            share = jnp.sum(jnp.where(eye, w / total, 0.0), axis=1, keepdims=True)
            out = out + share * p
        rows[g] = out
        for e in range(HERE):
            low = (g * HERE + e) * HEAD_DIM
            o_ref[:, low : low + HEAD_DIM] = rows[g, e * HOME : (e + 1) * HOME, :].astype(BF16)


def merge(x):
    return pl.pallas_call(
        merge_kernel,
        out_shape=jax.ShapeDtypeStruct((HOME, HEADS * HEAD_DIM), BF16),
        in_specs=[IN_VMEM],
        out_specs=IN_VMEM,
        scratch_shapes=[pltpu.VMEM((NG + 1, CHUNK, HEAD_DIM), F32)],
        compiler_params=params(8),
    )(x)


def from_back(x, axis, size, back):
    return lax.ppermute(x, axis, [(i, (i + back) % size) for i in range(size)])


def exchange(x, axes):
    return lax.all_to_all(x, axes, split_axis=0, concat_axis=0, tiled=True)


def on_device(span_qkv, history_kv):
    place = jnp.stack([lax.axis_index(a) for a in FRAMES]).astype(jnp.int32)
    other = lambda x: from_back(x, "c", NC, 1)
    back = from_back(history_kv, "y", NY, 1)
    ahead = from_back(history_kv, "y", NY, NY - 1)
    near = [history_kv, other(history_kv), back, other(back), ahead, other(ahead)]
    keys = from_back(back[0], "y", NY, 1)
    values = from_back(ahead[1], "y", NY, NY - 1)
    hist = near + [keys, other(keys), values, other(values)]

    q, kv = pack(span_qkv)
    kv = after(exchange(kv, GROUPS), back, ahead)
    q = exchange(q, PLANE)
    span = sort_span([kv] + [from_back(kv, "y", NY, d) for d in range(1, NY)], keys, values)
    partial = attend(place, q, hist, [span, other(span)])
    return merge(exchange(partial, PLANE))


def solution(mesh):
    cut = Mesh(mesh.devices.reshape(NZ, NY, NC, 2, 4), FRAMES + GROUPS)
    in_specs = (P(None, FRAMES + GROUPS, None), P(None, FRAMES, GROUPS))
    out_specs = P(FRAMES + GROUPS, None)
    return jax.shard_map(
        on_device, mesh=cut, in_specs=in_specs, out_specs=out_specs, check_vma=False
    )
```

```python
import math

import jax
import jax.numpy as jnp
from jax import lax
from jax.experimental import pallas as pl
from jax.experimental.pallas import tpu as pltpu
from jax.sharding import Mesh, PartitionSpec as P

HEADS = 40
HEAD_DIM = 128
TOKENS = 2304
HIST = 6144
FRAME_LEN = 768

FRAMES = ("zh", "y", "c")
GROUPS = ("zl", "x")
PLANE = ("zh", "x", "zl")
NX, NZL = 4, 2
NZ, NY, NC, NG = 4, 4, 2, 8
HERE = HEADS // NG
WIDE = HERE * HEAD_DIM
HOME = TOKENS // (NZ * NY * NC * NG)
OWN = HOME * NG
HKEYS = HIST // (NZ * NY * NC)
NHIST = NY * NC * HKEYS
ROWS = HERE * HOME
CHUNK = 48
KV_CHUNK = 96
CHUNKS = NZ * NG
QROWS = CHUNKS * HOME
SKEYS = NY * NG * HOME
KEYS = NHIST + NC * SKEYS
PIECES = 10
HEAD_PARTS = ((0, 1), (1, 5))
SCALE = math.log2(math.e) / math.sqrt(HEAD_DIM)
F32, BF16 = jnp.float32, jnp.bfloat16


def params(mib):
    return pltpu.CompilerParams(vmem_limit_bytes=mib * 2**20)


IN_VMEM = pl.BlockSpec(memory_space=pltpu.VMEM)
IN_SMEM = pl.BlockSpec(memory_space=pltpu.SMEM)
IN_HBM = pl.BlockSpec(memory_space=pltpu.HBM)
ANYWHERE = pl.BlockSpec(memory_space=pl.ANY)


def group_of(m):
    return (m % NZL) * NX + m // NZL


def pack_kernel(x_ref, q_ref, kv_ref, q_rows, kv_rows):
    for g in range(NG):
        q_rows[g, ROWS:, :] = jnp.zeros((CHUNK - ROWS, HEAD_DIM), F32)
        kv_rows[g, 2 * ROWS :, :] = jnp.zeros((KV_CHUNK - 2 * ROWS, HEAD_DIM), F32)
        for e in range(HERE):
            cols = slice((g * HERE + e) * HEAD_DIM, (g * HERE + e + 1) * HEAD_DIM)
            low = e * HOME
            q_rows[g, low : low + HOME, :] = x_ref[0, :, cols].astype(F32)
            kv_rows[g, low : low + HOME, :] = x_ref[1, :, cols].astype(F32)
            low += ROWS
            kv_rows[g, low : low + HOME, :] = x_ref[2, :, cols].astype(F32)
        q = q_rows[g].astype(BF16)
        member = (g % NX) * NZL + g // NX
        for z in range(NZ):
            q_ref[z * NG + member] = q
        kv_ref[g] = kv_rows[g].astype(BF16)


def pack(x):
    return pl.pallas_call(
        pack_kernel,
        out_shape=(
            jax.ShapeDtypeStruct((NZ * NG, CHUNK, HEAD_DIM), BF16),
            jax.ShapeDtypeStruct((NG, KV_CHUNK, HEAD_DIM), BF16),
        ),
        in_specs=[IN_VMEM],
        out_specs=(IN_VMEM, IN_VMEM),
        scratch_shapes=[
            pltpu.VMEM((NG + 1, CHUNK, HEAD_DIM), F32),
            pltpu.VMEM((NG + 1, KV_CHUNK, HEAD_DIM), F32),
        ],
        compiler_params=params(8),
    )(x)


def after_kernel(x_ref, *refs):
    refs[-1][...] = x_ref[...]


def after(x, *others):
    return pl.pallas_call(
        after_kernel,
        out_shape=jax.ShapeDtypeStruct(x.shape, x.dtype),
        in_specs=[IN_VMEM] + [ANYWHERE] * len(others),
        out_specs=IN_VMEM,
        compiler_params=params(8),
    )(x, *others)


def sort_kernel(*refs):
    o_ref, chunks, rows, sems = refs[-4:]
    copies = []
    for n in range(NY):
        where = chunks.at[pl.ds(n * NG, NG)]
        copies.append(pltpu.make_async_copy(refs[n], where, sems.at[n]))
    for copy in copies:
        copy.start()
    for copy in copies:
        copy.wait()
    rows[: CHUNKS * KV_CHUNK, :] = (
        chunks[...].astype(F32).reshape(CHUNKS * KV_CHUNK, HEAD_DIM)
    )
    for i in range(2):
        for e in range(HERE):
            for t in range(HOME):
                row = (i * HERE + e) * HOME + t
                o_ref[i, t * CHUNKS : (t + 1) * CHUNKS, e * HEAD_DIM : (e + 1) * HEAD_DIM] = rows[
                    pl.ds(row, CHUNKS, stride=KV_CHUNK), :
                ].astype(BF16)


def sort_span(span, *after):
    return pl.pallas_call(
        sort_kernel,
        out_shape=jax.ShapeDtypeStruct((2, SKEYS, WIDE), BF16),
        in_specs=[ANYWHERE] * (NY + len(after)),
        out_specs=IN_VMEM,
        scratch_shapes=[
            pltpu.VMEM((CHUNKS, KV_CHUNK, HEAD_DIM), BF16),
            pltpu.VMEM(((CHUNKS + 1) * KV_CHUNK, HEAD_DIM), F32),
            pltpu.SemaphoreType.DMA((NY,)),
        ],
        compiler_params=params(8),
        cost_estimate=pl.CostEstimate(flops=0, bytes_accessed=0, transcendentals=0),
    )(*span, *after)


def against(queries, keys):
    return lax.dot_general(
        queries, keys, (((1,), (1,)), ((), ())), preferred_element_type=F32
    )


def attend_kernel(place, q_ref, *refs):
    o_ref, kv_all, q_all, rows, sems = refs[PIECES + NC :]
    k_ref, v_ref = kv_all.at[0], kv_all.at[1]
    copies = []
    for n, (low, high) in enumerate(HEAD_PARTS):
        cols = pl.ds(low * HEAD_DIM, (high - low) * HEAD_DIM)
        moves = []
        for m in range(6):
            moves.append((refs[m].at[:, :, cols], kv_all.at[:, pl.ds(m * HKEYS, HKEYS), cols]))
        for m in range(2):
            where = pl.ds((6 + m) * HKEYS, HKEYS)
            moves.append((refs[6 + m].at[:, cols], k_ref.at[where, cols]))
            moves.append((refs[8 + m].at[:, cols], v_ref.at[where, cols]))
        for b in range(NC):
            where = pl.ds(NHIST + b * SKEYS, SKEYS)
            moves.append((refs[PIECES + b].at[:, :, cols], kv_all.at[:, where, cols]))
        copies.append(
            [pltpu.make_async_copy(x, to, sems.at[n, m]) for m, (x, to) in enumerate(moves)]
        )
        for copy in copies[n]:
            copy.start()
    rows[: CHUNKS * CHUNK, :] = q_ref[...].astype(F32).reshape(CHUNKS * CHUNK, HEAD_DIM)
    for e in range(HERE):
        for t in range(HOME):
            row = e * HOME + t
            q_all[e, t * CHUNKS : (t + 1) * CHUNKS, :] = rows[
                pl.ds(row, CHUNKS, stride=CHUNK), :
            ].astype(BF16)

    zh, y, c = place[0], place[1], place[2]
    row = lax.broadcasted_iota(jnp.int32, (QROWS, 1), 0)
    sender = lax.rem(row, CHUNKS)
    index = ((sender // NG) * NY + y) * NC + c
    member = lax.rem(sender, NG)
    group = lax.rem(member, NZL) * NX + member // NZL
    q_token = index * OWN + group * HOME + row // CHUNKS
    q_frame = q_token // FRAME_LEN
    col = lax.broadcasted_iota(jnp.int32, (1, NC * SKEYS), 1)
    core = jnp.where(col < SKEYS, c, 1 - c)
    col = lax.rem(col, SKEYS)
    sender = lax.rem(col, CHUNKS)
    index = (zh * NY + lax.rem(y + NY - sender // NG, NY)) * NC + core
    k_token = index * OWN + lax.rem(sender, NG) * HOME + col // CHUNKS
    k_frame = k_token // FRAME_LEN

    lane = lax.broadcasted_iota(jnp.int32, (CHUNKS, HEAD_DIM), 1)
    lses = jnp.zeros((CHUNKS, HEAD_DIM), F32)
    starts = {low: copies[n] for n, (low, high) in enumerate(HEAD_PARTS)}
    upcoming = None
    for e in range(HERE):
        for copy in starts.get(e, []) if e == 0 else []:
            copy.wait()
        score = against(q_all[0], k_ref[:, :HEAD_DIM]) if e == 0 else upcoming
        for copy in starts.get(e + 1, []):
            copy.wait()
        if e + 1 < HERE:
            upcoming = against(q_all[e + 1], k_ref[:, (e + 1) * HEAD_DIM : (e + 2) * HEAD_DIM])
        s_hist = score[:, :NHIST]
        s_span = jnp.where(q_frame >= k_frame, score[:, NHIST:], -1e30)
        top = jnp.maximum(
            jnp.max(s_hist, axis=1, keepdims=True), jnp.max(s_span, axis=1, keepdims=True)
        )
        weight = jnp.exp2((jnp.concatenate([s_hist, s_span], axis=1) - top) * SCALE)
        total = jnp.sum(weight, axis=1, keepdims=True)
        values = v_ref[:, e * HEAD_DIM : (e + 1) * HEAD_DIM]
        summed = jnp.dot(weight.astype(BF16), values, preferred_element_type=F32)
        partial = summed / total
        lse = top * SCALE + jnp.log2(total)
        for t in range(HOME):
            here = slice(t * CHUNKS, (t + 1) * CHUNKS)
            row = e * HOME + t
            rows[pl.ds(row, CHUNKS, stride=CHUNK), :] = partial[here]
            lses = jnp.where(lane == row, lse[here], lses)

    high = lses.astype(BF16).astype(F32)
    middle = (lses - high).astype(BF16).astype(F32)
    for n, term in enumerate((high, middle, lses - high - middle)):
        rows[pl.ds(ROWS + n, CHUNKS, stride=CHUNK), :] = term
    chunks = rows[: CHUNKS * CHUNK, :].reshape(CHUNKS, CHUNK, HEAD_DIM)
    o_ref[...] = chunks.astype(BF16)


def attend(place, q, hist, spans):
    return pl.pallas_call(
        attend_kernel,
        out_shape=jax.ShapeDtypeStruct((CHUNKS, CHUNK, HEAD_DIM), BF16),
        in_specs=[IN_SMEM, IN_VMEM] + [ANYWHERE] * (PIECES + NC),
        out_specs=IN_VMEM,
        scratch_shapes=[
            pltpu.VMEM((2, KEYS, WIDE), BF16),
            pltpu.VMEM((HERE, QROWS, HEAD_DIM), BF16),
            pltpu.VMEM(((CHUNKS + 1) * CHUNK, HEAD_DIM), F32),
            pltpu.SemaphoreType.DMA((len(HEAD_PARTS), PIECES + NC)),
        ],
        compiler_params=params(24),
        cost_estimate=pl.CostEstimate(
            flops=4 * QROWS * KEYS * WIDE,
            bytes_accessed=4 * KEYS * WIDE,
            transcendentals=QROWS * KEYS * HERE,
        ),
    )(place, q, *hist, *spans)


def merge_kernel(x_ref, o_ref, rows):
    eye = lax.broadcasted_iota(jnp.int32, (CHUNK, HEAD_DIM), 0) == lax.broadcasted_iota(
        jnp.int32, (CHUNK, HEAD_DIM), 1
    )
    for m in range(NG):
        g = group_of(m)
        parts = [x_ref[z * NG + m].astype(F32) for z in range(NZ)]
        lses = [
            (p[ROWS : ROWS + 1] + p[ROWS + 1 : ROWS + 2]) + p[ROWS + 2 : ROWS + 3] for p in parts
        ]
        top = jnp.maximum(jnp.maximum(lses[0], lses[1]), jnp.maximum(lses[2], lses[3]))
        weights = [jnp.exp2(v - top) for v in lses]
        total = (weights[0] + weights[1]) + (weights[2] + weights[3])
        out = jnp.zeros((CHUNK, HEAD_DIM), F32)
        for p, w in zip(parts, weights):
            share = jnp.sum(jnp.where(eye, w / total, 0.0), axis=1, keepdims=True)
            out = out + share * p
        rows[g] = out
        for e in range(HERE):
            low = (g * HERE + e) * HEAD_DIM
            o_ref[:, low : low + HEAD_DIM] = rows[g, e * HOME : (e + 1) * HOME, :].astype(BF16)


def merge(x):
    return pl.pallas_call(
        merge_kernel,
        out_shape=jax.ShapeDtypeStruct((HOME, HEADS * HEAD_DIM), BF16),
        in_specs=[IN_VMEM],
        out_specs=IN_VMEM,
        scratch_shapes=[pltpu.VMEM((NG + 1, CHUNK, HEAD_DIM), F32)],
        compiler_params=params(8),
    )(x)


def from_back(x, axis, size, back):
    return lax.ppermute(x, axis, [(i, (i + back) % size) for i in range(size)])


def exchange(x, axes):
    return lax.all_to_all(x, axes, split_axis=0, concat_axis=0, tiled=True)


def on_device(span_qkv, history_kv):
    place = jnp.stack([lax.axis_index(a) for a in FRAMES]).astype(jnp.int32)
    other = lambda x: from_back(x, "c", NC, 1)
    back = from_back(history_kv, "y", NY, 1)
    ahead = from_back(history_kv, "y", NY, NY - 1)
    near = [history_kv, other(history_kv), back, other(back), ahead, other(ahead)]
    keys = from_back(back[0], "y", NY, 1)
    values = from_back(ahead[1], "y", NY, NY - 1)
    hist = near + [keys, other(keys), values, other(values)]

    q, kv = pack(span_qkv)
    kv = after(exchange(kv, GROUPS), back, ahead)
    q = exchange(q, PLANE)
    span = sort_span([kv] + [from_back(kv, "y", NY, d) for d in range(1, NY)], keys, values)
    partial = attend(place, q, hist, [span, other(span)])
    return merge(exchange(partial, PLANE))


def solution(mesh):
    cut = Mesh(mesh.devices.reshape(NZ, NY, NC, 2, 4), FRAMES + GROUPS)
    in_specs = (P(None, FRAMES + GROUPS, None), P(None, FRAMES, GROUPS))
    out_specs = P(FRAMES + GROUPS, None)
    return jax.shard_map(
        on_device, mesh=cut, in_specs=in_specs, out_specs=out_specs, check_vma=False
    )
```
